256 devices in a mesh: fem: 16 (over z_hi, y), row: 4 (over x), col: 4 (over z_lo, core).
Axes of the slice: x: 4, y: 4, z: 8 (z_hi: 4, z_lo: 2; z = z_hi * 2 + z_lo), core: 2. Of those that a mesh axis runs over, the one named last changes fastest.
Arguments:
- inverse_factor: bfloat16 [256, 1536, 1536], P(('fem', 'row', 'col')), may hold values from -1 to 1.5, as said below
- coupling: bfloat16 [256, 1536, 1024], P(('fem', 'row', 'col')), may hold values from -0.19921875 to 0.19921875
- boundary_tiles: int32 [256, 8], replicated, may hold values from 0 to 15, as said below
- bem_block: float32 [1, 64, 128, 8192], P(None, ('fem', 'row'), None, 'col'), may hold values from -6 to 48
Outputs:
- boundary_factors: float32 [1, 64, 128, 8192], P(None, ('fem', 'row'), None, 'col')
The draws below stay inside these ranges and needn't reach their ends.
Inputs may be any that keep to these rules, and one draw needn't show every extreme that they name: `inverse_factor`: lower triangular. `boundary_tiles`: each row holds 8 distinct values.
All inputs are finite; a program needn't handle non-finite values.
Results may differ from the reference program's by a relative error of at most 0.0003.
Values may be sent and summed in bfloat16 or wider, within the bound.
A program may use at most 128 MiB of HBM per device.

```python
import math
import jax
import jax.numpy as jnp
from jax import lax

NB = 8192
TILE = 128
FEMDOF = 1536
BROWS = 1024
PW = 256
PANELS = 1
SUBS = 256
NFR = 64
KC = 1
QN = 16
SLOTS = 8
N_ROW = 4
N_COL = 4


def draw_inverse_factor(key, part):
    subkeys = jax.random.split(jax.random.fold_in(key, 11), SUBS)

    def single(subkey):
        first_key, second_key = jax.random.split(subkey)
        values = jnp.clip(jax.random.normal(first_key, (FEMDOF, FEMDOF), jnp.float32), -6.0, 6.0)
        values = values / math.sqrt(FEMDOF)
        diagonal = jax.random.uniform(second_key, (FEMDOF,), jnp.float32, 0.5, 1.5)
        return (jnp.tril(values, -1) + jnp.diag(diagonal)).astype(jnp.bfloat16)
    return lax.map(single, subkeys)


def draw_boundary_tiles(key, part):
    subkeys = jax.random.split(jax.random.fold_in(key, 23), SUBS)

    def single(subkey):
        return jax.random.permutation(subkey, QN)[:SLOTS].astype(jnp.int32)
    return jax.vmap(single)(subkeys)


def draw_bem_block(key, part):
    first_key, second_key = jax.random.split(jax.random.fold_in(key, 37))
    values = jnp.clip(jax.random.normal(first_key, (NB, NB), jnp.float32), -6.0, 6.0)
    diagonal = jax.random.uniform(second_key, (NB,), jnp.float32, 32.0, 48.0)
    indices = jnp.arange(NB)
    values = values.at[indices, indices].set(diagonal)
    return values.reshape(KC, NFR, TILE, NB)


def steps_of(own_key, shape, shards, least, high):
    def one(dim, shards_of):
        draws = jax.random.uniform(jax.random.fold_in(jax.random.fold_in(own_key, 6), dim), (shards_of,), jnp.float32, least / len(shards), high / len(shards))
        return jnp.repeat(jnp.exp(draws), shape[dim] // shards_of).reshape((-1,) + (1,) * (len(shape) - dim - 1))

    level = one(*shards[0])
    for cut in shards[1:]:
        level = level * one(*cut)
    return level


def centred(own_key, shape, deviation, bound, shards=(), kind=jnp.bfloat16):
    array = deviation * jax.random.normal(own_key, shape, jnp.float32)
    if shards:
        array = array * steps_of(own_key, shape, shards, -0.22, 0.18)
    return jnp.clip(array, -bound, bound).astype(kind)


def setup_inputs(seed: int = 0) -> dict:
    arg_keys = jax.random.split(jax.random.key(seed), 5)
    inverse_factor = draw_inverse_factor(jax.random.fold_in(arg_keys[4], 71), 0)
    coupling = centred(arg_keys[1], (SUBS, FEMDOF, BROWS), 0.03, 0.19921875, ((0, 256),))
    boundary_tiles = draw_boundary_tiles(jax.random.fold_in(arg_keys[4], 71), 0)
    bem_block = draw_bem_block(jax.random.fold_in(arg_keys[4], 71), 0)
    return dict(inverse_factor=inverse_factor, coupling=coupling, boundary_tiles=boundary_tiles, bem_block=bem_block)


def factor(square):
    extent = square.shape[0]
    if extent <= 16:
        for column in range(extent - 1):
            scaled = square[column + 1:, column] / square[column, column]
            square = square.at[column + 1:, column].set(scaled)
            square = square.at[column + 1:, column + 1:].add(-scaled[:, None] * square[column, column + 1:][None, :])
        return square
    halfway = extent // 2
    leading = factor(square[:halfway, :halfway])
    lower_part = jnp.tril(leading, -1) + jnp.eye(halfway, dtype=square.dtype)
    upper_part = jnp.triu(leading)
    right_part = jax.scipy.linalg.solve_triangular(lower_part, square[:halfway, halfway:], lower=True, unit_diagonal=True)
    below_part = jax.scipy.linalg.solve_triangular(upper_part, square[halfway:, :halfway].T, trans=1, lower=False).T
    remainder = factor(square[halfway:, halfway:] - jnp.dot(below_part, right_part, precision=lax.Precision.HIGHEST))
    top_half = jnp.concatenate([leading, right_part], axis=1)
    bottom_half = jnp.concatenate([below_part, remainder], axis=1)
    return jnp.concatenate([top_half, bottom_half], axis=0)

def reference(inverse_factor, coupling, boundary_tiles, bem_block):
    offsets = jnp.arange(TILE, dtype=jnp.int32)
    residue = (jnp.arange(SUBS, dtype=jnp.int32) // N_COL % N_ROW).astype(jnp.int32)

    def accumulate(carried, inputs):
        factor_sub, coupling_sub, tiles_sub, residue_sub = inputs
        coupled = jnp.dot(factor_sub.astype(jnp.float32), coupling_sub.astype(jnp.float32), preferred_element_type=jnp.float32).astype(jnp.bfloat16)
        rounded = jnp.dot(coupled.T.astype(jnp.float32), coupled.astype(jnp.float32), preferred_element_type=jnp.float32).astype(jnp.bfloat16)
        contribution = lax.optimization_barrier(rounded).astype(jnp.float32)
        indices = ((N_ROW * tiles_sub + residue_sub)[:, None] * TILE + offsets[None, :]).reshape(-1).astype(jnp.int32)
        carried = carried.at[indices[:, None], indices[None, :]].add(contribution)
        return (carried, None)
    assembled, _ = lax.scan(accumulate, jnp.zeros((NB, NB), jnp.float32), (inverse_factor, coupling, boundary_tiles, residue))
    boundary = bem_block.reshape(NB, NB) + assembled
    for panel in range(PANELS):
        start_col = panel * PW
        stop_col = start_col + PW
        packed = factor(boundary[start_col:stop_col, start_col:stop_col])
        lower_unit = jnp.tril(packed, -1) + jnp.eye(PW, dtype=packed.dtype)
        upper_part = jnp.triu(packed)
        upper_rows = jax.scipy.linalg.solve_triangular(lower_unit, boundary[start_col:stop_col, stop_col:], lower=True, unit_diagonal=True)
        lower_rows = jax.scipy.linalg.solve_triangular(upper_part, boundary[stop_col:, start_col:stop_col].T, trans=1, lower=False).T
        update = jnp.dot(lower_rows, upper_rows, precision=lax.Precision.HIGHEST)
        boundary = boundary.at[stop_col:, stop_col:].set(boundary[stop_col:, stop_col:] - update)
        boundary = boundary.at[start_col:stop_col, stop_col:].set(upper_rows)
        boundary = boundary.at[stop_col:, start_col:stop_col].set(lower_rows)
        boundary = boundary.at[start_col:stop_col, start_col:stop_col].set(packed)
    return boundary.reshape(bem_block.shape)
```

```python
import jax
import jax.numpy as jnp
from jax import lax
from jax.experimental import pallas as pl
from jax.experimental.pallas import tpu as pltpu
from jax.sharding import PartitionSpec as P

MESH = pl.DeviceIdType.MESH
F32 = jnp.float32
BF16 = jnp.bfloat16
T = 128
VMEM_LIMIT = 60 * 1024 * 1024


def highest(left, right):
    return jnp.dot(left, right, precision=lax.Precision.HIGHEST, preferred_element_type=F32)


def contribution_kernel(place_ref, factor_ref, coupling_ref, out_ref, coupled):
    order, width = coupling_ref.shape
    step = 256
    out_ref[...] = jnp.zeros_like(out_ref)
    for i in range(order // step):
        for n in range(width // 512):
            coupled[i * step : (i + 1) * step, n * 512 : (n + 1) * 512] = jnp.dot(
                factor_ref[i * step : (i + 1) * step, : (i + 1) * step],
                coupling_ref[: (i + 1) * step, n * 512 : (n + 1) * 512],
                preferred_element_type=F32,
            ).astype(BF16)
    for pair in range(width // step):
        for n in range(width // 512):
            block = lax.dot_general(
                coupled[:, pair * step : (pair + 1) * step],
                coupled[:, n * 512 : (n + 1) * 512],
                (((0,), (0,)), ((), ())),
                preferred_element_type=F32,
            ).astype(BF16)
            for half in range(step // T):
                place = place_ref[pair * (step // T) + half]
                for j in range(512 // T):
                    out_ref[place, n * (512 // T) + j] = block[
                        half * T : (half + 1) * T, j * T : (j + 1) * T
                    ]


def contribution(places, factor, coupling, tiles):
    order, width = coupling.shape
    slots = width // T
    return pl.pallas_call(
        contribution_kernel,
        out_shape=jax.ShapeDtypeStruct((tiles, slots, T, T), BF16),
        in_specs=[
            pl.BlockSpec(memory_space=pltpu.SMEM),
            pl.BlockSpec(memory_space=pltpu.VMEM),
            pl.BlockSpec(memory_space=pltpu.VMEM),
        ],
        out_specs=pl.BlockSpec(memory_space=pltpu.VMEM),
        scratch_shapes=[pltpu.VMEM((order, width), BF16)],
        compiler_params=pltpu.CompilerParams(vmem_limit_bytes=VMEM_LIMIT),
        name="contribution",
    )(places, factor, coupling)


def assemble_kernel(
    slot_ref, weight_ref, dense_ref, bem_ref,
    m_ref, panel_ref, diag_ref, cols_ref,
    recv, acc, other, plus0, minus0, plus, minus, xpart, ypart, zpart,
    y_send, y_recv, c_send, c_recv, r_send, r_recv,
    px_send, px_recv, py_send, py_recv, pz_send, pz_recv,
    gy_send, gy_recv, gx_send, gx_recv, d_send, d_recv, a_send, a_recv,
):
    f = lax.axis_index("fem")
    r = lax.axis_index("row")
    c = lax.axis_index("col")
    zh, y = f // 4, f % 4
    zl, core = c // 2, c % 2
    z = zh * 2 + zl

    def at_y(d):
        return (zh * 4 + (y + d) % 4, r, c)

    def at_z(d):
        to = (z + d + 8) % 8
        return ((to // 2) * 4 + y, r, (to % 2) * 2 + core)

    def at_zh(d):
        return (((zh + d) % 4) * 4 + y, r, c)

    def at_x(d):
        return (f, (r + d) % 4, c)

    def at_col(d):
        return (f, r, (c + d) % 4)

    partner = (f, r, c + 1 - 2 * core)

    def copy(src, dst, send, recv_sem, to):
        return pltpu.make_async_remote_copy(
            src_ref=src, dst_ref=dst, send_sem=send, recv_sem=recv_sem,
            device_id=to, device_id_type=MESH,
        )

    barrier = pltpu.get_barrier_semaphore()
    greet = [at_y(d) for d in (1, 2, 3)] + [at_z(1), at_z(-1)]
    greet += [at_zh(d) for d in (1, 2, 3)] + [at_x(d) for d in (1, 2, 3)]
    greet += [at_col(d) for d in (1, 2, 3)]
    for to in greet:
        pl.semaphore_signal(barrier, inc=1, device_id=to, device_id_type=MESH)
    pl.semaphore_wait(barrier, len(greet))

    y_copies = []
    for q in range(4):
        for d in (1, 2, 3):
            one = copy(
                dense_ref.at[q * 4 + (y + d) % 4], recv.at[d - 1, q],
                y_send.at[d - 1, q], y_recv.at[d - 1, q], at_y(d),
            )
            one.start()
            y_copies.append(one)
    for one in y_copies:
        one.wait()

    def gather(step, carry):
        q = step // 4
        b4 = step % 4
        side = (b4 % 2 + core) % 2
        zto = q * 2 + b4 // 2
        for i in range(4):
            b = b4 * 4 + i
            total = dense_ref[q * 4 + y, slot_ref[b]].astype(F32) * weight_ref[b]
            for d in (1, 2, 3):
                total += recv[d - 1, q, slot_ref[d * 16 + b]].astype(F32) * weight_ref[d * 16 + b]
            acc[side, zto, :, i * T : (i + 1) * T] = total
        return carry

    lax.fori_loop(0, 16, gather, 0)

    swap = copy(acc.at[1], other, c_send, c_recv, partner)
    swap.start()
    swap.wait()

    half = T // 2
    far = (z + 4) % 8
    acc[0, far] = acc[0, far] + other[far]
    ring = []

    def hop(src, dst, lane, d):
        one = copy(src, dst, r_send.at[lane, d], r_recv.at[lane, d], at_z(1 - 2 * lane))
        one.start()
        ring.append(one)
        return one

    up = hop(acc.at[0, far, pl.ds(0, half)], plus0, 0, 0)
    down = hop(acc.at[0, far, pl.ds(half, half)], minus0, 1, 0)
    for d in (3, 2, 1):
        zp = (z + d) % 8
        zm = (z + 8 - d) % 8
        acc[0, zp] = acc[0, zp] + other[zp]
        acc[0, zm] = acc[0, zm] + other[zm]
        up.wait_recv()
        if d == 3:
            acc[0, zp, 0:half] = acc[0, zp, 0:half] + plus0[...]
        else:
            acc[0, zp] = acc[0, zp] + plus[2 - d]
        up = hop(acc.at[0, zp], plus.at[3 - d], 0, 4 - d)
        down.wait_recv()
        if d == 3:
            acc[0, zm, half:T] = acc[0, zm, half:T] + minus0[...]
        else:
            acc[0, zm] = acc[0, zm] + minus[2 - d]
        down = hop(acc.at[0, zm], minus.at[3 - d], 1, 4 - d)
    m_ref[...] = bem_ref[...]
    up.wait_recv()
    down.wait_recv()
    for i in range(4):
        lanes = pl.ds(pl.multiple_of((i * 4 + r) * T, T), T)
        part = pl.ds(i * T, T)
        m_ref[:, lanes] = m_ref[:, lanes] + (
            acc[0, z, :, part] + other[z, :, part] + plus[2, :, part] + minus[2, :, part]
        )
    for one in ring:
        one.wait_send()

    def col_copies():
        return [
            copy(m_ref.at[:, pl.ds(0, 256)], cols_ref, a_send.at[d - 1], a_recv, at_col(d))
            for d in (1, 2, 3)
        ]

    @pl.when(c == 0)
    def _():
        for one in col_copies():
            one.start()

    def x_copies():
        return [
            copy(
                m_ref.at[:, pl.ds(pl.multiple_of(((r + d) % 4) * 512, 512), 512)], xpart.at[r % 2],
                px_send.at[d - 1], px_recv.at[r % 2], at_x(d),
            )
            for d in (1, 2, 3)
        ]

    def y_parts():
        return [
            copy(
                xpart.at[:, pl.ds(d * 32, 32)], ypart, py_send.at[d - 1], py_recv, (d, r, c)
            )
            for d in (1, 2, 3)
        ]

    def z_parts():
        return [copy(ypart, ypart, pz_send.at[d - 1], pz_recv, at_zh(d)) for d in (1, 2, 3)]

    @pl.when(f == 0)
    def _():
        @pl.when(r < 2)
        def _():
            for one in x_copies():
                one.start()
            xpart[r % 2] = m_ref[:, pl.ds(pl.multiple_of((r % 2) * 512, 512), 512)]

        for m in range(2):
            @pl.when(r != m)
            def _():
                copy(xpart.at[m], xpart.at[m], px_send.at[0], px_recv.at[m], at_x(1)).wait_recv()

        for one in y_parts():
            one.start()
        ypart[...] = xpart[:, 0:32]

    @pl.when((zh == 0) & (y != 0))
    def _():
        copy(ypart, ypart, py_send.at[0], py_recv, at_x(1)).wait_recv()

    @pl.when(zh == 0)
    def _():
        for one in z_parts():
            one.start()

    @pl.when(zh != 0)
    def _():
        copy(ypart, ypart, pz_send.at[0], pz_recv, at_x(1)).wait_recv()

    rows = pl.ds(pl.multiple_of(y * 32, 32), 32)
    gy = [
        copy(ypart, zpart.at[:, rows], gy_send.at[d - 1], gy_recv.at[d - 1], at_y(d))
        for d in (1, 2, 3)
    ]
    for one in gy:
        one.start()
    zpart[:, rows] = ypart[...]
    for one in gy:
        one.wait_recv()
    gx = [
        copy(zpart, panel_ref.at[r], gx_send.at[d - 1], gx_recv.at[d - 1], at_x(d))
        for d in (1, 2, 3)
    ]
    for one in gx:
        one.start()
    panel_ref[r] = zpart[...]
    for one in gx:
        one.wait_recv()

    def diag_copies():
        return [
            copy(panel_ref.at[0, :, :, pl.ds(0, 256)], diag_ref, d_send.at[d - 1], d_recv, at_col(d))
            for d in (1, 2, 3)
        ]

    @pl.when(c == 0)
    def _():
        for one in diag_copies():
            one.start()
        diag_ref[...] = panel_ref[0, :, :, 0:256]
        cols_ref[...] = m_ref[:, 0:256]
        for one in diag_copies() + col_copies():
            one.wait_send()

    @pl.when(c != 0)
    def _():
        copy(cols_ref, cols_ref, a_send.at[0], a_recv, at_col(1)).wait_recv()
        copy(diag_ref, diag_ref, d_send.at[0], d_recv, at_col(1)).wait_recv()

    @pl.when(f == 0)
    def _():
        @pl.when(r < 2)
        def _():
            for one in x_copies():
                one.wait_send()

        for one in y_parts():
            one.wait_send()

    @pl.when(zh == 0)
    def _():
        for one in z_parts():
            one.wait_send()

    for one in gy + gx:
        one.wait_send()


def assemble(slots, weights, dense, bem):
    vmem = pl.BlockSpec(memory_space=pltpu.VMEM)
    smem = pl.BlockSpec(memory_space=pltpu.SMEM)
    dma = pltpu.SemaphoreType.DMA
    return pl.pallas_call(
        assemble_kernel,
        out_shape=[
            jax.ShapeDtypeStruct((T, 2048), F32),
            jax.ShapeDtypeStruct((4, 2, T, 512), F32),
            jax.ShapeDtypeStruct((2, T, 256), F32),
            jax.ShapeDtypeStruct((T, 256), F32),
        ],
        in_specs=[smem, smem, vmem, vmem],
        out_specs=[vmem, vmem, vmem, vmem],
        scratch_shapes=[
            pltpu.VMEM((3, 4, 8, T, T), BF16),
            pltpu.VMEM((2, 8, T, 512), F32),
            pltpu.VMEM((8, T, 512), F32),
            pltpu.VMEM((T // 2, 512), F32),
            pltpu.VMEM((T // 2, 512), F32),
            pltpu.VMEM((3, T, 512), F32),
            pltpu.VMEM((3, T, 512), F32),
            pltpu.VMEM((2, T, 512), F32),
            pltpu.VMEM((2, 32, 512), F32),
            pltpu.VMEM((2, T, 512), F32),
            dma((3, 4)), dma((3, 4)), dma, dma, dma((2, 4)), dma((2, 4)),
            dma((3,)), dma((2,)), dma((3,)), dma, dma((3,)), dma,
            dma((3,)), dma((3,)), dma((3,)), dma((3,)), dma((3,)), dma, dma((3,)), dma,
        ],
        compiler_params=pltpu.CompilerParams(
            collective_id=0, has_side_effects=True, vmem_limit_bytes=VMEM_LIMIT
        ),
        name="assemble",
    )(slots, weights, dense, bem)


def eliminate(work, unit, first, last):
    lanes = lax.broadcasted_iota(jnp.int32, (1, T), 1)
    for j in range(T):
        top = (j // 8) * 8
        count = last - top
        row = work[j : j + 1, :]
        inverse_pivot = 1.0 / row[:, j : j + 1]
        below = lax.broadcasted_iota(jnp.int32, (count, 1), 0) + top > j
        block = work[top:last, :]
        scaled = jnp.where(below, block[:, j : j + 1] * inverse_pivot, 0.0)
        right = jnp.where(lanes > j, row, 0.0)
        work[top:last, :] = jnp.where(
            (lanes == j) & below, scaled, block - scaled * right
        )
        unit[top:T, :] = unit[top:T, :] - scaled[: T - top] * unit[j : j + 1, :]


def update_kernel(m_ref, panel_ref, diag_ref, cols_ref, out_ref, work, unit):
    f = lax.axis_index("fem")
    r = lax.axis_index("row")
    c = lax.axis_index("col")
    identity = (
        lax.broadcasted_iota(jnp.int32, (T, T), 0) == lax.broadcasted_iota(jnp.int32, (T, T), 1)
    ).astype(F32)
    work[0:T, :] = diag_ref[0, :, 0:T]
    work[T : 2 * T, :] = diag_ref[1, :, 0:T]
    work[2 * T : 3 * T, :] = cols_ref[:, 0:T]
    unit[...] = identity
    eliminate(work, unit, 0, 3 * T)
    first = work[...]
    first_inv = unit[...]
    upper = highest(first_inv, diag_ref[0, :, T:256])
    work[0:T, :] = diag_ref[1, :, T:256] - highest(first[T : 2 * T], upper)
    work[T : 2 * T, :] = cols_ref[:, T:256] - highest(first[2 * T :], upper)
    unit[...] = identity
    eliminate(work, unit, 0, 2 * T)
    second = work[0 : 2 * T, :]
    second_inv = unit[...]
    corner = -highest(second_inv, highest(first[T : 2 * T], first_inv))
    lower = second[T:]
    is_panel = (f == 0) & (r < 2)
    left = jnp.where(
        is_panel,
        jnp.where(r == 0, first_inv, corner),
        -(highest(first[2 * T :], first_inv) + highest(lower, corner)),
    )
    right = jnp.where(
        is_panel,
        jnp.where(r == 0, jnp.zeros_like(second_inv), second_inv),
        -highest(lower, second_inv),
    )
    keep = jnp.where(is_panel, 0.0, 1.0).astype(F32)
    for n in range(4):
        cut = pl.ds(n * 512, 512)
        out_ref[:, cut] = (
            m_ref[:, cut] * keep
            + highest(left, panel_ref[n, 0])
            + highest(right, panel_ref[n, 1])
        )

    @pl.when(c == 0)
    def _():
        out_ref[:, 0:T] = jnp.where(
            is_panel, jnp.where(r == 0, first[0:T], first[T : 2 * T]), first[2 * T :]
        )
        out_ref[:, T:256] = jnp.where(
            is_panel, jnp.where(r == 0, upper, second[0:T]), lower
        )


def update(matrix, panel, diag, cols):
    vmem = pl.BlockSpec(memory_space=pltpu.VMEM)
    return pl.pallas_call(
        update_kernel,
        out_shape=jax.ShapeDtypeStruct(matrix.shape, F32),
        in_specs=[vmem] * 4,
        out_specs=vmem,
        scratch_shapes=[pltpu.VMEM((3 * T, T), F32), pltpu.VMEM((T, T), F32)],
        compiler_params=pltpu.CompilerParams(vmem_limit_bytes=VMEM_LIMIT),
        name="update",
    )(matrix, panel, diag, cols)


def local(inverse_factor, coupling, boundary_tiles, bem_block):
    f = lax.axis_index("fem")
    r = lax.axis_index("row")
    c = lax.axis_index("col")
    rows = lax.axis_size("row")
    columns = lax.axis_size("col")
    tiles = lax.axis_size("fem")
    y = f % 4
    sources = (((f // 4) * 4 + (y - jnp.arange(4)) % 4) * rows + r) * columns + c
    lists = boundary_tiles[sources]
    match = lists[:, :, None] == jnp.arange(tiles, dtype=jnp.int32)[None, None, :]
    slots = jnp.sum(
        jnp.where(match, jnp.arange(lists.shape[1], dtype=jnp.int32)[None, :, None], 0), axis=1
    ).reshape(-1)
    weights = jnp.any(match, axis=1).astype(F32).reshape(-1)
    dense = contribution(lists[0], inverse_factor[0], coupling[0], tiles)
    matrix, panel, diag, cols = assemble(slots, weights, dense, bem_block[0, 0])
    return update(matrix, panel, diag, cols)[None, None]


def solution(mesh):
    placed = (
        P(("fem", "row", "col"), None, None),
        P(("fem", "row", "col"), None, None),
        P(),
        P(None, ("fem", "row"), None, "col"),
    )
    return jax.shard_map(
        local,
        mesh=mesh,
        in_specs=placed,
        out_specs=P(None, ("fem", "row"), None, "col"),
        check_vma=False,
    )
```

```python
import jax
import jax.numpy as jnp
from jax import lax
from jax.experimental import pallas as pl
from jax.experimental.pallas import tpu as pltpu
from jax.sharding import PartitionSpec as P

MESH = pl.DeviceIdType.MESH
F32 = jnp.float32
BF16 = jnp.bfloat16
T = 128
VMEM_LIMIT = 60 * 1024 * 1024


def highest(left, right):
    return jnp.dot(left, right, precision=lax.Precision.HIGHEST, preferred_element_type=F32)


def contribution_kernel(
    tiles_ref, factor_ref, coupling_ref, out_ref, slot_ref, weight_ref, coupled
):
    f = lax.axis_index("fem")
    r = lax.axis_index("row")
    c = lax.axis_index("col")
    order, width = coupling_ref.shape
    tiles, slots = out_ref.shape[0], out_ref.shape[1]
    step = 256
    for i in range(4 * tiles):
        slot_ref[i] = 0
        weight_ref[i] = 0.0
    for d in range(4):
        source = (((f // 4) * 4 + (f + 4 - d) % 4) * 4 + r) * 4 + c
        for k in range(slots):
            tile = tiles_ref[source, k]
            slot_ref[d * tiles + tile] = k
            weight_ref[d * tiles + tile] = 1.0
    me = (f * 4 + r) * 4 + c
    out_ref[...] = jnp.zeros_like(out_ref)
    for i in range(order // step):
        for n in range(width // 512):
            coupled[i * step : (i + 1) * step, n * 512 : (n + 1) * 512] = jnp.dot(
                factor_ref[i * step : (i + 1) * step, : (i + 1) * step],
                coupling_ref[: (i + 1) * step, n * 512 : (n + 1) * 512],
                preferred_element_type=F32,
            ).astype(BF16)
    for pair in range(width // step):
        for n in range(width // 512):
            block = lax.dot_general(
                coupled[:, pair * step : (pair + 1) * step],
                coupled[:, n * 512 : (n + 1) * 512],
                (((0,), (0,)), ((), ())),
                preferred_element_type=F32,
            ).astype(BF16)
            for half in range(step // T):
                place = tiles_ref[me, pair * (step // T) + half]
                for j in range(512 // T):
                    out_ref[place, n * (512 // T) + j] = block[
                        half * T : (half + 1) * T, j * T : (j + 1) * T
                    ]


def contribution(boundary_tiles, factor, coupling, tiles):
    order, width = coupling.shape
    slots = width // T
    smem = pl.BlockSpec(memory_space=pltpu.SMEM)
    vmem = pl.BlockSpec(memory_space=pltpu.VMEM)
    return pl.pallas_call(
        contribution_kernel,
        out_shape=[
            jax.ShapeDtypeStruct((tiles, slots, T, T), BF16),
            jax.ShapeDtypeStruct((4 * tiles,), jnp.int32),
            jax.ShapeDtypeStruct((4 * tiles,), F32),
        ],
        in_specs=[smem, vmem, vmem],
        out_specs=[vmem, smem, smem],
        scratch_shapes=[pltpu.VMEM((order, width), BF16)],
        compiler_params=pltpu.CompilerParams(vmem_limit_bytes=VMEM_LIMIT),
        name="contribution",
    )(boundary_tiles, factor, coupling)


def eliminate_part(work, unit, part, last):
    lanes = lax.broadcasted_iota(jnp.int32, (1, T), 1)
    top = part * 32
    count = last - top
    place = lax.broadcasted_iota(jnp.int32, (count, 1), 0) + top

    def block(step, carry):
        start = pl.multiple_of(top + step * 8, 8)
        for t in range(8):
            row = work[pl.ds(start + t, 1), :]
            unit_row = unit[pl.ds(start + t, 1), :]
            inverse_pivot = 1.0 / row[:, t : t + 1]
            below = place > start + t
            body = work[top:last, :]
            scaled = jnp.where(below, body[:, t : t + 1] * inverse_pivot, 0.0)
            right = jnp.where((lanes > t) & (lanes < T - start), row, 0.0)
            work[top:last, :] = jnp.where((lanes == t) & below, scaled, body - scaled * right)
            unit[top:T, :] = unit[top:T, :] - scaled[: T - top] * unit_row
        work[top:last, :] = pltpu.roll(work[top:last, :], T - 8, 1)
        return carry

    lax.fori_loop(0, 4, block, 0)


def turn_back(work):
    for part in range(3):
        cut = slice(part * 32, (part + 1) * 32)
        work[cut, :] = pltpu.roll(work[cut, :], (part + 1) * 32, 1)


def solve_kernel(
    slot_ref, weight_ref, dense_ref, bem_ref,
    out_ref,
    recv0, recv1, recv2, recv3, acc, other, plus0, minus0, plus, minus,
    xpart, ypart, zpart, panel,
    prow, psum, pother, pz, piece, pa32, pa, atile,
    dy32, d8, gq, g32, diag, cols,
    work, unit,
    y_send, y_recv, c_send, c_recv, r_send, r_recv,
    px_send, px_recv, py_send, py_recv, pz_send, pz_recv, gy_send, gy_recv, gx_send, gx_recv,
    b1_send, b1_recv, b2_send, b2_recv, b3_send, b3_recv, b4_send, b4_recv, b5_send, b5_recv,
    b6_send, b6_recv, at_send, at_recv,
    e1_send, e1_recv, e2_send, e2_recv, q0_send, q0_recv, q1_send, q1_recv,
    q2_send, q2_recv, q3_send, q3_recv, a_send, a_recv,
):
    f = lax.axis_index("fem")
    r = lax.axis_index("row")
    c = lax.axis_index("col")
    zh, y = f // 4, f % 4
    zl, core = c // 2, c % 2
    z = zh * 2 + zl
    three = (1, 2, 3)
    recv = (recv0, recv1, recv2, recv3)

    def at_y(d):
        return (zh * 4 + (y + d) % 4, r, c)

    def at_z(d):
        to = (z + d) % 8
        return ((to // 2) * 4 + y, r, (to % 2) * 2 + core)

    def at_zh(d):
        return (((zh + d) % 4) * 4 + y, r, c)

    def at_x(d):
        return (f, (r + d) % 4, c)

    def at_col(d):
        return (f, r, (c + d) % 4)

    partner = (f, r, c + 1 - 2 * core)

    def copy(src, dst, send, recv_sem, to):
        return pltpu.make_async_remote_copy(
            src_ref=src, dst_ref=dst, send_sem=send, recv_sem=recv_sem,
            device_id=to, device_id_type=MESH,
        )

    def arrive(dst, recv_sem):
        copy(dst, dst, recv_sem, recv_sem, at_x(1)).wait_recv()

    def start(copies):
        for one in copies:
            one.start()

    def rows_of(index, count):
        return pl.ds(pl.multiple_of(index * count, count), count)

    barrier = pltpu.get_barrier_semaphore()
    greet = [at_y(d) for d in three] + [at_z(d) for d in range(1, 8)]
    greet += [at_x(d) for d in three] + [at_col(d) for d in three]
    for to in greet:
        pl.semaphore_signal(barrier, inc=1, device_id=to, device_id_type=MESH)
    pl.semaphore_wait(barrier, len(greet))

    in_panel = r < 2
    is_root = (f == 0) & in_panel
    mine = r % 2

    b1 = [
        copy(
            dense_ref.at[0, :, rows_of((y + d) % 4, 32)], prow.at[d - 1],
            b1_send.at[d - 1], b1_recv.at[d - 1], at_y(d),
        )
        for d in three
    ]
    e1 = [
        copy(
            bem_ref.at[pl.ds(d * 32, 32), pl.ds(0, 256)], dy32, e1_send.at[d - 1], e1_recv,
            (d, r, c),
        )
        for d in three
    ]
    e2 = [
        copy(
            dy32.at[rows_of((zh + d) % 4, 8)], d8, e2_send.at[d - 1], e2_recv, at_zh(d)
        )
        for d in three
    ]
    a_copies = [
        copy(bem_ref.at[:, pl.ds(0, 256)], cols, a_send.at[d - 1], a_recv, at_col(d))
        for d in three
    ]
    px = [
        copy(
            bem_ref.at[:, rows_of((r + d) % 4, 512)], xpart.at[mine],
            px_send.at[d - 1], px_recv.at[mine], at_x(d),
        )
        for d in three
    ]

    @pl.when(in_panel)
    def _():
        start(b1)

        @pl.when(f == 0)
        def _():
            @pl.when(c == 0)
            def _():
                start(e1)
                dy32[...] = bem_ref[0:32, 0:256]

            start(px)
            xpart[mine] = bem_ref[:, rows_of(mine, 512)]

    @pl.when(c == 0)
    def _():
        start(a_copies)
        cols[...] = bem_ref[:, 0:256]

    rounds = (2, 1, 3, 0)
    tile_row = [(zh + turn) % 4 for turn in rounds]
    y_copies = [
        [
            copy(
                dense_ref.at[tile_row[k] * 4 + (y + d) % 4], recv[k].at[d - 1],
                y_send.at[d - 1, k], y_recv.at[d - 1, k], at_y(d),
            )
            for d in three
        ]
        for k in range(4)
    ]
    start(y_copies[0])

    b2 = copy(psum.at[1], pother, b2_send, b2_recv, partner)
    b3 = [
        copy(
            psum.at[0, ((z + d) % 8) % 2, rows_of(((z + d) % 8) // 2, 8)], pz.at[d - 1],
            b3_send.at[d - 1], b3_recv.at[d - 1], at_z(d),
        )
        for d in range(1, 8)
    ]

    @pl.when(in_panel & (c == 0))
    def _():
        @pl.when(zh == 0)
        def _():
            @pl.when(y != 0)
            def _():
                arrive(dy32, e1_recv)

            start(e2)
            d8[...] = dy32[0:8]

    @pl.when(in_panel)
    def _():
        for one in b1:
            one.wait_recv()

        def add_row(b4, carry):
            for i in range(4):
                b = b4 * 4 + i
                total = (
                    dense_ref[0, slot_ref[b], rows_of(y, 32)].astype(F32) * weight_ref[b]
                )
                for d in three:
                    total += (
                        prow[d - 1, slot_ref[d * 16 + b]].astype(F32) * weight_ref[d * 16 + b]
                    )
                psum[(b4 % 2 + core) % 2, b4 // 2, :, i * T : (i + 1) * T] = total
            return carry

        lax.fori_loop(0, 4, add_row, 0)
        b2.start()

    py = [
        copy(xpart.at[:, pl.ds(d * 32, 32)], ypart, py_send.at[d - 1], py_recv, (d, r, c))
        for d in three
    ]
    pzs = [copy(ypart, ypart, pz_send.at[d - 1], pz_recv, at_zh(d)) for d in three]

    @pl.when(f == 0)
    def _():
        for m in range(2):
            @pl.when(r != m)
            def _():
                arrive(xpart.at[m], px_recv.at[m])

        start(py)
        ypart[...] = xpart[:, 0:32]

    @pl.when(in_panel)
    def _():
        b2.wait_recv()
        psum[0] = psum[0] + pother[...]
        start(b3)

    start(y_copies[1])

    @pl.when(zh == 0)
    def _():
        @pl.when(y != 0)
        def _():
            arrive(ypart, py_recv)

        start(pzs)

    q0 = [copy(gq.at[mine], gq.at[mine], q0_send.at[d - 1], q0_recv, at_col(d)) for d in three]
    q1 = [
        copy(gq.at[mine], gq.at[mine], q1_send.at[d - 1], q1_recv.at[mine], at_x(d))
        for d in three
    ]
    b4 = [
        copy(piece, pa32.at[rows_of(zh, 8)], b4_send.at[d - 1], b4_recv.at[d - 1], at_zh(d))
        for d in three
    ]

    @pl.when(in_panel)
    def _():
        for one in b3:
            one.wait_recv()
        total = psum[0, zl, rows_of(zh, 8)]
        for d in range(7):
            total += pz[d]
        piece[...] = total
        start(b4)
        pa32[rows_of(zh, 8)] = total

        @pl.when(c == 0)
        def _():
            @pl.when(zh != 0)
            def _():
                arrive(d8, e2_recv)

            for m in range(2):
                @pl.when(r == m)
                def _():
                    gq[m, :, (1 - m) * T : (2 - m) * T] = d8[:, (1 - m) * T : (2 - m) * T]
                    gq[m, :, m * T : (m + 1) * T] = d8[:, m * T : (m + 1) * T] + total[:, 0:T]

            start(q0)

        @pl.when(c != 0)
        def _():
            arrive(gq.at[mine], q0_recv)

        start(q1)

    q2 = [
        copy(gq, g32.at[:, rows_of(zh, 8)], q2_send.at[d - 1], q2_recv.at[d - 1], at_zh(d))
        for d in three
    ]
    q3 = [
        copy(g32, diag.at[:, rows_of(y, 32)], q3_send.at[d - 1], q3_recv.at[d - 1], at_y(d))
        for d in three
    ]
    b5 = [
        copy(pa32, pa.at[mine, rows_of(y, 32)], b5_send.at[d - 1], b5_recv.at[d - 1], at_y(d))
        for d in three
    ]
    b6 = [
        copy(pa.at[mine], pa.at[mine], b6_send.at[d - 1], b6_recv.at[mine], at_x(d))
        for d in three
    ]
    tile_lanes = rows_of(f % 4, T)
    at_copies = [
        copy(pa.at[mine, :, tile_lanes], atile, at_send.at[d - 1], at_recv, at_col(d))
        for d in three
    ]
    for m in range(2):
        @pl.when(r != m)
        def _():
            arrive(gq.at[m], q1_recv.at[m])

    start(q2)
    g32[:, rows_of(zh, 8)] = gq[...]

    @pl.when(in_panel)
    def _():
        for one in b4:
            one.wait_recv()
        start(b5)
        pa[mine, rows_of(y, 32)] = pa32[...]

    for one in q2:
        one.wait_recv()
    start(q3)
    diag[:, rows_of(y, 32)] = g32[...]

    gy = [
        copy(ypart, zpart.at[:, rows_of(y, 32)], gy_send.at[d - 1], gy_recv.at[d - 1], at_y(d))
        for d in three
    ]
    gx = [
        copy(zpart, panel.at[r], gx_send.at[d - 1], gx_recv.at[d - 1], at_x(d)) for d in three
    ]

    @pl.when(zh != 0)
    def _():
        arrive(ypart, pz_recv)

    start(gy)
    zpart[:, rows_of(y, 32)] = ypart[...]

    swaps = [
        copy(
            acc.at[1, rows_of(tile_row[k], 2)], other.at[rows_of(tile_row[k], 2)],
            c_send.at[k], c_recv.at[k], partner,
        )
        for k in range(4)
    ]

    def add_round(k):
        for one in y_copies[k]:
            one.wait_recv()
        q = tile_row[k]

        def gather(b4, carry):
            for i in range(4):
                b = b4 * 4 + i
                total = dense_ref[q * 4 + y, slot_ref[b]].astype(F32) * weight_ref[b]
                for d in three:
                    total += (
                        recv[k][d - 1, slot_ref[d * 16 + b]].astype(F32) * weight_ref[d * 16 + b]
                    )
                acc[(b4 % 2 + core) % 2, q * 2 + b4 // 2, :, i * T : (i + 1) * T] = total
            return carry

        lax.fori_loop(0, 4, gather, 0)
        swaps[k].start()

    half = T // 2
    ring = []

    def hop(src, dst, lane, d):
        one = copy(src, dst, r_send.at[lane, d], r_recv.at[lane, d], at_z(1 + 6 * lane))
        one.start()
        ring.append(one)
        return one

    def first_hop():
        swaps[0].wait_recv()
        far = (z + 4) % 8
        acc[0, far] = acc[0, far] + other[far]
        return (
            hop(acc.at[0, far, pl.ds(0, half)], plus0, 0, 0),
            hop(acc.at[0, far, pl.ds(half, half)], minus0, 1, 0),
        )

    def next_hop(d, up, down):
        zp = (z + d) % 8
        zm = (z + 8 - d) % 8
        acc[0, zp] = acc[0, zp] + other[zp]
        acc[0, zm] = acc[0, zm] + other[zm]
        up.wait_recv()
        if d == 3:
            acc[0, zp, 0:half] = acc[0, zp, 0:half] + plus0[...]
        else:
            acc[0, zp] = acc[0, zp] + plus[2 - d]
        up = hop(acc.at[0, zp], plus.at[3 - d], 0, 4 - d)
        down.wait_recv()
        if d == 3:
            acc[0, zm, half:T] = acc[0, zm, half:T] + minus0[...]
        else:
            acc[0, zm] = acc[0, zm] + minus[2 - d]
        down = hop(acc.at[0, zm], minus.at[3 - d], 1, 4 - d)
        return up, down

    add_round(0)

    @pl.when(in_panel)
    def _():
        for one in b5:
            one.wait_recv()
        start(b6)

        @pl.when(c == f // 4)
        def _():
            start(at_copies)
            atile[...] = pa[mine, :, tile_lanes]

    start(y_copies[2])
    for one in gy:
        one.wait_recv()
    start(gx)
    panel[r] = zpart[...]
    for one in q3:
        one.wait_recv()

    @pl.when(c != 0)
    def _():
        arrive(cols, a_recv)

    @pl.when(in_panel)
    def _():
        @pl.when(c != f // 4)
        def _():
            arrive(atile, at_recv)

        turned = atile[...].T
        for m in range(2):
            @pl.when(r == m)
            def _():
                cols[:, m * T : (m + 1) * T] = cols[:, m * T : (m + 1) * T] + turned

    identity = (
        lax.broadcasted_iota(jnp.int32, (T, T), 0) == lax.broadcasted_iota(jnp.int32, (T, T), 1)
    ).astype(F32)
    work[0:T, :] = diag[0, :, 0:T]
    work[T : 2 * T, :] = diag[1, :, 0:T]
    work[2 * T : 3 * T, :] = cols[:, 0:T]
    unit[...] = identity
    eliminate_part(work, unit, 0, 3 * T)
    up, down = first_hop()
    eliminate_part(work, unit, 1, 3 * T)
    start(y_copies[3])
    add_round(1)
    eliminate_part(work, unit, 2, 3 * T)
    eliminate_part(work, unit, 3, 3 * T)
    turn_back(work)
    first = work[...]
    first_inv = unit[...]
    upper = highest(first_inv, diag[0, :, T:256])
    add_round(2)
    swaps[1].wait_recv()
    swaps[2].wait_recv()
    up, down = next_hop(3, up, down)
    work[0:T, :] = diag[1, :, T:256] - highest(first[T : 2 * T], upper)
    work[T : 2 * T, :] = cols[:, T:256] - highest(first[2 * T :], upper)
    unit[...] = identity
    eliminate_part(work, unit, 0, 2 * T)
    eliminate_part(work, unit, 1, 2 * T)
    up, down = next_hop(2, up, down)
    eliminate_part(work, unit, 2, 2 * T)
    add_round(3)
    eliminate_part(work, unit, 3, 2 * T)
    turn_back(work)
    swaps[3].wait_recv()
    up, down = next_hop(1, up, down)

    second = work[0 : 2 * T, :]
    second_inv = unit[...]
    corner = -highest(second_inv, highest(first[T : 2 * T], first_inv))
    lower = second[T:]
    left = jnp.where(
        is_root,
        jnp.where(r == 0, first_inv, corner),
        -(highest(first[2 * T :], first_inv) + highest(lower, corner)),
    )
    right = jnp.where(
        is_root,
        jnp.where(r == 0, jnp.zeros_like(second_inv), second_inv),
        -highest(lower, second_inv),
    )
    keep = jnp.where(is_root, 0.0, 1.0).astype(F32)
    for one in gx:
        one.wait_recv()
    for m in range(2):
        @pl.when(r != m)
        def _():
            arrive(pa.at[m], b6_recv.at[m])

    for n in range(4):
        for m in range(2):
            panel[n, m, :, m * T : (m + 1) * T] = (
                panel[n, m, :, m * T : (m + 1) * T] + pa[m, :, n * T : (n + 1) * T]
            )
    for n in range(4):
        cut = pl.ds(n * 512, 512)
        out_ref[:, cut] = (
            bem_ref[:, cut] * keep + highest(left, panel[n, 0]) + highest(right, panel[n, 1])
        )

    up.wait_recv()
    down.wait_recv()
    for i in range(4):
        lanes = pl.ds(pl.multiple_of((i * 4 + r) * T, T), T)
        part = pl.ds(i * T, T)
        out_ref[:, lanes] = out_ref[:, lanes] + keep * (
            acc[0, z, :, part] + other[z, :, part] + plus[2, :, part] + minus[2, :, part]
        )

    @pl.when(c == 0)
    def _():
        out_ref[:, 0:T] = jnp.where(
            is_root, jnp.where(r == 0, first[0:T], first[T : 2 * T]), first[2 * T :]
        )
        out_ref[:, T:256] = jnp.where(
            is_root, jnp.where(r == 0, upper, second[0:T]), lower
        )

    def sent(copies):
        for one in copies:
            one.wait_send()

    sent(ring + swaps + gy + gx + q2 + q3)
    for k in range(4):
        sent(y_copies[k])

    @pl.when(in_panel)
    def _():
        sent(b1 + [b2] + b3 + b4 + b5 + b6 + q1)

        @pl.when(c == 0)
        def _():
            sent(q0)

            @pl.when(zh == 0)
            def _():
                sent(e2)

        @pl.when(f == 0)
        def _():
            sent(px)

            @pl.when(c == 0)
            def _():
                sent(e1)

        @pl.when(c == f // 4)
        def _():
            sent(at_copies)

    @pl.when(c == 0)
    def _():
        sent(a_copies)

    @pl.when(f == 0)
    def _():
        sent(py)

    @pl.when(zh == 0)
    def _():
        sent(pzs)


def solve(slots, weights, dense, bem):
    vmem = pl.BlockSpec(memory_space=pltpu.VMEM)
    smem = pl.BlockSpec(memory_space=pltpu.SMEM)
    dma = pltpu.SemaphoreType.DMA
    f32 = lambda *shape: pltpu.VMEM(shape, F32)
    return pl.pallas_call(
        solve_kernel,
        out_shape=jax.ShapeDtypeStruct(bem.shape, F32),
        in_specs=[smem, smem, vmem, vmem],
        out_specs=vmem,
        scratch_shapes=[
            *[pltpu.VMEM((3, 8, T, T), BF16)] * 4,
            f32(2, 8, T, 512),
            f32(8, T, 512),
            f32(T // 2, 512), f32(T // 2, 512), f32(3, T, 512), f32(3, T, 512),
            f32(2, T, 512), f32(2, 32, 512), f32(2, T, 512), f32(4, 2, T, 512),
            pltpu.VMEM((3, 8, 32, T), BF16),
            f32(2, 2, 32, 512), f32(2, 32, 512), f32(7, 8, 512), f32(8, 512), f32(32, 512),
            f32(2, T, 512), f32(T, T),
            f32(32, 256), f32(8, 256), f32(2, 8, 256), f32(2, 32, 256), f32(2, T, 256),
            f32(T, 256),
            f32(3 * T, T), f32(T, T),
            dma((3, 4)), dma((3, 4)), dma((4,)), dma((4,)), dma((2, 4)), dma((2, 4)),
            dma((3,)), dma((2,)), dma((3,)), dma, dma((3,)), dma,
            dma((3,)), dma((3,)), dma((3,)), dma((3,)),
            dma((3,)), dma((3,)), dma, dma, dma((7,)), dma((7,)), dma((3,)), dma((3,)),
            dma((3,)), dma((3,)),
            dma((3,)), dma((2,)), dma((3,)), dma,
            dma((3,)), dma, dma((3,)), dma, dma((3,)), dma, dma((3,)), dma((2,)),
            dma((3,)), dma((3,)), dma((3,)), dma((3,)), dma((3,)), dma,
        ],
        compiler_params=pltpu.CompilerParams(
            collective_id=0, has_side_effects=True, vmem_limit_bytes=VMEM_LIMIT
        ),
        name="solve",
    )(slots, weights, dense, bem)


def local(inverse_factor, coupling, boundary_tiles, bem_block):
    tiles = lax.axis_size("fem")
    dense, slots, weights = contribution(boundary_tiles, inverse_factor[0], coupling[0], tiles)
    return solve(slots, weights, dense, bem_block[0, 0])[None, None]


def solution(mesh):
    placed = (
        P(("fem", "row", "col"), None, None),
        P(("fem", "row", "col"), None, None),
        P(),
        P(None, ("fem", "row"), None, "col"),
    )
    return jax.shard_map(
        local,
        mesh=mesh,
        in_specs=placed,
        out_specs=P(None, ("fem", "row"), None, "col"),
        check_vma=False,
    )
```

```python
import jax
import jax.numpy as jnp
from jax import lax
from jax.experimental import pallas as pl
from jax.experimental.pallas import tpu as pltpu
from jax.sharding import PartitionSpec as P

MESH = pl.DeviceIdType.MESH
F32 = jnp.float32
BF16 = jnp.bfloat16
T = 128
VMEM_LIMIT = 60 * 1024 * 1024


def highest(left, right):
    return jnp.dot(left, right, precision=lax.Precision.HIGHEST, preferred_element_type=F32)


def eliminate_part(work, unit, part, last):
    lanes = lax.broadcasted_iota(jnp.int32, (1, T), 1)
    top = part * 32
    count = last - top
    place = lax.broadcasted_iota(jnp.int32, (count, 1), 0) + top

    def block(step, carry):
        start = pl.multiple_of(top + step * 8, 8)
        for t in range(8):
            row = work[pl.ds(start + t, 1), :]
            unit_row = unit[pl.ds(start + t, 1), :]
            inverse_pivot = 1.0 / row[:, t : t + 1]
            below = place > start + t
            body = work[top:last, :]
            scaled = jnp.where(below, body[:, t : t + 1] * inverse_pivot, 0.0)
            right = jnp.where((lanes > t) & (lanes < T - start), row, 0.0)
            work[top:last, :] = jnp.where((lanes == t) & below, scaled, body - scaled * right)
            unit[top:T, :] = unit[top:T, :] - scaled[: T - top] * unit_row
        work[top:last, :] = pltpu.roll(work[top:last, :], T - 8, 1)
        return carry

    lax.fori_loop(0, 4, block, 0)


def turn_back(work):
    for part in range(3):
        cut = slice(part * 32, (part + 1) * 32)
        work[cut, :] = pltpu.roll(work[cut, :], (part + 1) * 32, 1)


def solve_kernel(
    tiles_ref, factor_ref, coupling_ref, bem_ref,
    out_ref,
    slot_ref, weight_ref, factor, coupling, coupled, compact, dense_ref, f_sem, k_sem,
    recv0, recv1, recv2, recv3, acc, other, plus0, minus0, plus, minus,
    xpart, ypart, zpart, panel,
    prow, psum, pother, pz, piece, pa32, pa, atile,
    dy32, d8, gq, g32, diag, cols,
    work, unit,
    y_send, y_recv, c_send, c_recv, r_send, r_recv,
    px_send, px_recv, py_send, py_recv, pz_send, pz_recv, gy_send, gy_recv, gx_send, gx_recv,
    b1_send, b1_recv, b2_send, b2_recv, b3_send, b3_recv, b4_send, b4_recv, b5_send, b5_recv,
    b6_send, b6_recv, at_send, at_recv,
    e1_send, e1_recv, e2_send, e2_recv, q0_send, q0_recv, q1_send, q1_recv,
    q2_send, q2_recv, q3_send, q3_recv, a_send, a_recv,
):
    f = lax.axis_index("fem")
    r = lax.axis_index("row")
    c = lax.axis_index("col")
    zh, y = f // 4, f % 4
    zl, core = c // 2, c % 2
    z = zh * 2 + zl
    three = (1, 2, 3)
    recv = (recv0, recv1, recv2, recv3)

    def at_y(d):
        return (zh * 4 + (y + d) % 4, r, c)

    def at_z(d):
        to = (z + d) % 8
        return ((to // 2) * 4 + y, r, (to % 2) * 2 + core)

    def at_zh(d):
        return (((zh + d) % 4) * 4 + y, r, c)

    def at_x(d):
        return (f, (r + d) % 4, c)

    def at_col(d):
        return (f, r, (c + d) % 4)

    partner = (f, r, c + 1 - 2 * core)

    def copy(src, dst, send, recv_sem, to):
        return pltpu.make_async_remote_copy(
            src_ref=src, dst_ref=dst, send_sem=send, recv_sem=recv_sem,
            device_id=to, device_id_type=MESH,
        )

    def arrive(dst, recv_sem):
        copy(dst, dst, recv_sem, recv_sem, at_x(1)).wait_recv()

    def start(copies):
        for one in copies:
            one.start()

    def rows_of(index, count):
        return pl.ds(pl.multiple_of(index * count, count), count)

    order, width = coupling.shape
    step = 256
    loads = []
    for i in range(order // step):
        block = pl.ds(i * step, step)
        left_part = pl.ds(0, (i + 1) * step)
        loads.append(
            (
                pltpu.make_async_copy(
                    factor_ref.at[block, left_part], factor.at[block, left_part], f_sem.at[i]
                ),
                pltpu.make_async_copy(coupling_ref.at[block], coupling.at[block], k_sem.at[i]),
            )
        )
        start(loads[i])

    barrier = pltpu.get_barrier_semaphore()
    greet = [at_y(d) for d in three] + [at_z(d) for d in range(1, 8)]
    greet += [at_x(d) for d in three] + [at_col(d) for d in three]
    for to in greet:
        pl.semaphore_signal(barrier, inc=1, device_id=to, device_id_type=MESH)
    pl.semaphore_wait(barrier, len(greet))

    in_panel = r < 2
    is_root = (f == 0) & in_panel
    mine = r % 2

    b1 = [
        copy(
            dense_ref.at[0, :, rows_of((y + d) % 4, 32)], prow.at[d - 1],
            b1_send.at[d - 1], b1_recv.at[d - 1], at_y(d),
        )
        for d in three
    ]
    e1 = [
        copy(
            bem_ref.at[pl.ds(d * 32, 32), pl.ds(0, 256)], dy32, e1_send.at[d - 1], e1_recv,
            (d, r, c),
        )
        for d in three
    ]
    e2 = [
        copy(
            dy32.at[rows_of((zh + d) % 4, 8)], d8, e2_send.at[d - 1], e2_recv, at_zh(d)
        )
        for d in three
    ]
    a_copies = [
        copy(bem_ref.at[:, pl.ds(0, 256)], cols, a_send.at[d - 1], a_recv, at_col(d))
        for d in three
    ]
    px = [
        copy(
            bem_ref.at[:, rows_of((r + d) % 4, 512)], xpart.at[mine],
            px_send.at[d - 1], px_recv.at[mine], at_x(d),
        )
        for d in three
    ]

    @pl.when(is_root)
    def _():
        @pl.when(c == 0)
        def _():
            start(e1)
            dy32[...] = bem_ref[0:32, 0:256]

        start(px)
        xpart[mine] = bem_ref[:, rows_of(mine, 512)]

    @pl.when(c == 0)
    def _():
        start(a_copies)
        cols[...] = bem_ref[:, 0:256]

    rounds = (2, 1, 3, 0)
    tile_row = [(zh + turn) % 4 for turn in rounds]
    y_copies = [
        [
            copy(
                dense_ref.at[tile_row[k] * 4 + (y + d) % 4], recv[k].at[d - 1],
                y_send.at[d - 1, k], y_recv.at[d - 1, k], at_y(d),
            )
            for d in three
        ]
        for k in range(4)
    ]

    py = [
        copy(xpart.at[:, pl.ds(d * 32, 32)], ypart, py_send.at[d - 1], py_recv, (d, r, c))
        for d in three
    ]
    pzs = [copy(ypart, ypart, pz_send.at[d - 1], pz_recv, at_zh(d)) for d in three]

    gy = [
        copy(ypart, zpart.at[:, rows_of(y, 32)], gy_send.at[d - 1], gy_recv.at[d - 1], at_y(d))
        for d in three
    ]
    gx = [
        copy(zpart, panel.at[r], gx_send.at[d - 1], gx_recv.at[d - 1], at_x(d)) for d in three
    ]

    for d in range(4):
        source = ((zh * 4 + (y + 4 - d) % 4) * 4 + r) * 4 + c
        listed = [tiles_ref[source, k] for k in range(8)]

        def look(b, carry):
            slot = jnp.int32(0)
            weight = jnp.float32(0.0)
            for k in range(8):
                slot = jnp.where(listed[k] == b, k, slot)
                weight = jnp.where(listed[k] == b, jnp.float32(1.0), weight)
            slot_ref[d * 16 + b] = slot
            weight_ref[d * 16 + b] = weight
            return carry

        lax.fori_loop(0, 16, look, 0)

    for i in range(order // step):
        for one in loads[i]:
            one.wait()
        for n in range(width // 512):
            coupled[i * step : (i + 1) * step, n * 512 : (n + 1) * 512] = jnp.dot(
                factor[i * step : (i + 1) * step, : (i + 1) * step],
                coupling[: (i + 1) * step, n * 512 : (n + 1) * 512],
                preferred_element_type=F32,
            ).astype(BF16)

    @pl.when(in_panel & (c == 0))
    def _():
        @pl.when(zh == 0)
        def _():
            @pl.when(y != 0)
            def _():
                arrive(dy32, e1_recv)

            start(e2)
            d8[...] = dy32[0:8]

    @pl.when(f == 0)
    def _():
        for m in range(2):
            @pl.when(r != m)
            def _():
                arrive(xpart.at[m], px_recv.at[m])

        start(py)
        ypart[...] = xpart[:, 0:32]

    for pair in range(width // step):
        for n in range(width // 512):
            both = lax.dot_general(
                coupled[:, pair * step : (pair + 1) * step],
                coupled[:, n * 512 : (n + 1) * 512],
                (((0,), (0,)), ((), ())),
                preferred_element_type=F32,
            ).astype(BF16)
            for i in range(step // T):
                for j in range(512 // T):
                    compact[pair * (step // T) + i, n * (512 // T) + j] = both[
                        i * T : (i + 1) * T, j * T : (j + 1) * T
                    ]

    dense_ref[0] = compact[slot_ref[0]]

    @pl.when(in_panel)
    def _():
        start(b1)

    def place(b, carry):
        dense_ref[b] = compact[slot_ref[b]]
        return carry

    lax.fori_loop(1, 16, place, 0)
    start(y_copies[0])
    @pl.when(zh == 0)
    def _():
        @pl.when(y != 0)
        def _():
            arrive(ypart, py_recv)

        start(pzs)

    b2 = copy(psum.at[1], pother, b2_send, b2_recv, partner)
    b3 = [
        copy(
            psum.at[0, ((z + d) % 8) % 2, rows_of(((z + d) % 8) // 2, 8)], pz.at[d - 1],
            b3_send.at[d - 1], b3_recv.at[d - 1], at_z(d),
        )
        for d in range(1, 8)
    ]

    @pl.when(in_panel)
    def _():
        for one in b1:
            one.wait_recv()

        def add_row(b4, carry):
            for i in range(4):
                b = b4 * 4 + i
                total = compact[slot_ref[0], slot_ref[b], rows_of(y, 32)].astype(F32) * (
                    weight_ref[b] * weight_ref[0]
                )
                for d in three:
                    total += prow[d - 1, slot_ref[d * 16 + b]].astype(F32) * (
                        weight_ref[d * 16 + b] * weight_ref[d * 16]
                    )
                psum[(b4 % 2 + core) % 2, b4 // 2, :, i * T : (i + 1) * T] = total
            return carry

        lax.fori_loop(0, 4, add_row, 0)
        b2.start()

    @pl.when(in_panel)
    def _():
        b2.wait_recv()
        psum[0] = psum[0] + pother[...]
        start(b3)

    start(y_copies[1])
    @pl.when(zh != 0)
    def _():
        arrive(ypart, pz_recv)

    start(gy)
    zpart[:, rows_of(y, 32)] = ypart[...]


    q0 = [copy(gq.at[mine], gq.at[mine], q0_send.at[d - 1], q0_recv, at_col(d)) for d in three]
    q1 = [
        copy(gq.at[mine], gq.at[mine], q1_send.at[d - 1], q1_recv.at[mine], at_x(d))
        for d in three
    ]
    b4 = [
        copy(piece, pa32.at[rows_of(zh, 8)], b4_send.at[d - 1], b4_recv.at[d - 1], at_zh(d))
        for d in three
    ]

    @pl.when(in_panel)
    def _():
        for one in b3:
            one.wait_recv()
        total = psum[0, zl, rows_of(zh, 8)]
        for d in range(7):
            total += pz[d]
        piece[...] = total
        start(b4)
        pa32[rows_of(zh, 8)] = total

        @pl.when(c == 0)
        def _():
            @pl.when(zh != 0)
            def _():
                arrive(d8, e2_recv)

            for m in range(2):
                @pl.when(r == m)
                def _():
                    gq[m, :, (1 - m) * T : (2 - m) * T] = d8[:, (1 - m) * T : (2 - m) * T]
                    gq[m, :, m * T : (m + 1) * T] = d8[:, m * T : (m + 1) * T] + total[:, 0:T]

            start(q0)

        @pl.when(c != 0)
        def _():
            arrive(gq.at[mine], q0_recv)

        start(q1)

    q2 = [
        copy(gq, g32.at[:, rows_of(zh, 8)], q2_send.at[d - 1], q2_recv.at[d - 1], at_zh(d))
        for d in three
    ]
    q3 = [
        copy(g32, diag.at[:, rows_of(y, 32)], q3_send.at[d - 1], q3_recv.at[d - 1], at_y(d))
        for d in three
    ]
    b5 = [
        copy(pa32, pa.at[mine, rows_of(y, 32)], b5_send.at[d - 1], b5_recv.at[d - 1], at_y(d))
        for d in three
    ]
    b6 = [
        copy(pa.at[mine], pa.at[mine], b6_send.at[d - 1], b6_recv.at[mine], at_x(d))
        for d in three
    ]
    tile_lanes = rows_of(f % 4, T)
    at_copies = [
        copy(pa.at[mine, :, tile_lanes], atile, at_send.at[d - 1], at_recv, at_col(d))
        for d in three
    ]
    for m in range(2):
        @pl.when(r != m)
        def _():
            arrive(gq.at[m], q1_recv.at[m])

    start(q2)
    g32[:, rows_of(zh, 8)] = gq[...]

    @pl.when(in_panel)
    def _():
        for one in b4:
            one.wait_recv()
        start(b5)
        pa[mine, rows_of(y, 32)] = pa32[...]

    for one in q2:
        one.wait_recv()
    start(q3)
    diag[:, rows_of(y, 32)] = g32[...]
    start(y_copies[2])
    for one in gy:
        one.wait_recv()
    start(gx)
    panel[r] = zpart[...]

    swaps = [
        copy(
            acc.at[1, rows_of(tile_row[k], 2)], other.at[rows_of(tile_row[k], 2)],
            c_send.at[k], c_recv.at[k], partner,
        )
        for k in range(4)
    ]

    def add_round(k):
        for one in y_copies[k]:
            one.wait_recv()
        q = tile_row[k]
        row = q * 4 + y

        def gather(b4, carry):
            for i in range(4):
                b = b4 * 4 + i
                total = compact[slot_ref[row], slot_ref[b]].astype(F32) * (
                    weight_ref[b] * weight_ref[row]
                )
                for d in three:
                    total += recv[k][d - 1, slot_ref[d * 16 + b]].astype(F32) * (
                        weight_ref[d * 16 + b] * weight_ref[d * 16 + row]
                    )
                acc[(b4 % 2 + core) % 2, q * 2 + b4 // 2, :, i * T : (i + 1) * T] = total
            return carry

        lax.fori_loop(0, 4, gather, 0)
        swaps[k].start()

    half = T // 2
    ring = []

    def hop(src, dst, lane, d):
        one = copy(src, dst, r_send.at[lane, d], r_recv.at[lane, d], at_z(1 + 6 * lane))
        one.start()
        ring.append(one)
        return one

    def first_hop():
        swaps[0].wait_recv()
        far = (z + 4) % 8
        acc[0, far] = acc[0, far] + other[far]
        return (
            hop(acc.at[0, far, pl.ds(0, half)], plus0, 0, 0),
            hop(acc.at[0, far, pl.ds(half, half)], minus0, 1, 0),
        )

    def next_hop(d, up, down):
        zp = (z + d) % 8
        zm = (z + 8 - d) % 8
        acc[0, zp] = acc[0, zp] + other[zp]
        acc[0, zm] = acc[0, zm] + other[zm]
        up.wait_recv()
        if d == 3:
            acc[0, zp, 0:half] = acc[0, zp, 0:half] + plus0[...]
        else:
            acc[0, zp] = acc[0, zp] + plus[2 - d]
        up = hop(acc.at[0, zp], plus.at[3 - d], 0, 4 - d)
        down.wait_recv()
        if d == 3:
            acc[0, zm, half:T] = acc[0, zm, half:T] + minus0[...]
        else:
            acc[0, zm] = acc[0, zm] + minus[2 - d]
        down = hop(acc.at[0, zm], minus.at[3 - d], 1, 4 - d)
        return up, down

    add_round(0)

    @pl.when(in_panel)
    def _():
        for one in b5:
            one.wait_recv()
        start(b6)

        @pl.when(c == f // 4)
        def _():
            start(at_copies)
            atile[...] = pa[mine, :, tile_lanes]

    for one in q3:
        one.wait_recv()

    @pl.when(c != 0)
    def _():
        arrive(cols, a_recv)

    @pl.when(in_panel)
    def _():
        @pl.when(c != f // 4)
        def _():
            arrive(atile, at_recv)

        turned = atile[...].T
        for m in range(2):
            @pl.when(r == m)
            def _():
                cols[:, m * T : (m + 1) * T] = cols[:, m * T : (m + 1) * T] + turned

    start(y_copies[3])

    identity = (
        lax.broadcasted_iota(jnp.int32, (T, T), 0) == lax.broadcasted_iota(jnp.int32, (T, T), 1)
    ).astype(F32)
    work[0:T, :] = diag[0, :, 0:T]
    work[T : 2 * T, :] = diag[1, :, 0:T]
    work[2 * T : 3 * T, :] = cols[:, 0:T]
    unit[...] = identity
    eliminate_part(work, unit, 0, 3 * T)
    up, down = first_hop()
    eliminate_part(work, unit, 1, 3 * T)
    add_round(1)
    eliminate_part(work, unit, 2, 3 * T)
    eliminate_part(work, unit, 3, 3 * T)
    turn_back(work)
    first = work[...]
    first_inv = unit[...]
    upper = highest(first_inv, diag[0, :, T:256])
    add_round(2)
    swaps[1].wait_recv()
    swaps[2].wait_recv()
    up, down = next_hop(3, up, down)
    work[0:T, :] = diag[1, :, T:256] - highest(first[T : 2 * T], upper)
    work[T : 2 * T, :] = cols[:, T:256] - highest(first[2 * T :], upper)
    unit[...] = identity
    eliminate_part(work, unit, 0, 2 * T)
    eliminate_part(work, unit, 1, 2 * T)
    up, down = next_hop(2, up, down)
    eliminate_part(work, unit, 2, 2 * T)
    add_round(3)
    eliminate_part(work, unit, 3, 2 * T)
    turn_back(work)
    swaps[3].wait_recv()
    up, down = next_hop(1, up, down)

    second = work[0 : 2 * T, :]
    second_inv = unit[...]
    corner = -highest(second_inv, highest(first[T : 2 * T], first_inv))
    lower = second[T:]
    left = jnp.where(
        is_root,
        jnp.where(r == 0, first_inv, corner),
        -(highest(first[2 * T :], first_inv) + highest(lower, corner)),
    )
    right = jnp.where(
        is_root,
        jnp.where(r == 0, jnp.zeros_like(second_inv), second_inv),
        -highest(lower, second_inv),
    )
    keep = jnp.where(is_root, 0.0, 1.0).astype(F32)
    for one in gx:
        one.wait_recv()
    for m in range(2):
        @pl.when(r != m)
        def _():
            arrive(pa.at[m], b6_recv.at[m])

    for n in range(4):
        for m in range(2):
            panel[n, m, :, m * T : (m + 1) * T] = (
                panel[n, m, :, m * T : (m + 1) * T] + pa[m, :, n * T : (n + 1) * T]
            )
    for n in range(4):
        cut = pl.ds(n * 512, 512)
        out_ref[:, cut] = (
            bem_ref[:, cut] * keep + highest(left, panel[n, 0]) + highest(right, panel[n, 1])
        )

    up.wait_recv()
    down.wait_recv()
    for i in range(4):
        lanes = pl.ds(pl.multiple_of((i * 4 + r) * T, T), T)
        part = pl.ds(i * T, T)
        out_ref[:, lanes] = out_ref[:, lanes] + keep * (
            acc[0, z, :, part] + other[z, :, part] + plus[2, :, part] + minus[2, :, part]
        )

    @pl.when(c == 0)
    def _():
        out_ref[:, 0:T] = jnp.where(
            is_root, jnp.where(r == 0, first[0:T], first[T : 2 * T]), first[2 * T :]
        )
        out_ref[:, T:256] = jnp.where(
            is_root, jnp.where(r == 0, upper, second[0:T]), lower
        )

    def sent(copies):
        for one in copies:
            one.wait_send()

    sent(ring + swaps + gy + gx + q2 + q3)
    for k in range(4):
        sent(y_copies[k])

    @pl.when(in_panel)
    def _():
        sent(b1 + [b2] + b3 + b4 + b5 + b6 + q1)

        @pl.when(c == 0)
        def _():
            sent(q0)

            @pl.when(zh == 0)
            def _():
                sent(e2)

        @pl.when(f == 0)
        def _():
            sent(px)

            @pl.when(c == 0)
            def _():
                sent(e1)

        @pl.when(c == f // 4)
        def _():
            sent(at_copies)

    @pl.when(c == 0)
    def _():
        sent(a_copies)

    @pl.when(f == 0)
    def _():
        sent(py)

    @pl.when(zh == 0)
    def _():
        sent(pzs)


def solve(tiles, factor, coupling, bem):
    vmem = pl.BlockSpec(memory_space=pltpu.VMEM)
    smem = pl.BlockSpec(memory_space=pltpu.SMEM)
    dma = pltpu.SemaphoreType.DMA
    f32 = lambda *shape: pltpu.VMEM(shape, F32)
    return pl.pallas_call(
        solve_kernel,
        out_shape=jax.ShapeDtypeStruct(bem.shape, F32),
        in_specs=[smem, pl.BlockSpec(memory_space=pl.ANY), pl.BlockSpec(memory_space=pl.ANY), vmem],
        out_specs=vmem,
        scratch_shapes=[
            pltpu.SMEM((64,), jnp.int32), pltpu.SMEM((64,), F32),
            pltpu.VMEM(factor.shape, BF16), pltpu.VMEM(coupling.shape, BF16),
            pltpu.VMEM(coupling.shape, BF16),
            pltpu.VMEM((8, 8, T, T), BF16), pltpu.VMEM((16, 8, T, T), BF16),
            dma((6,)), dma((6,)),
            *[pltpu.VMEM((3, 8, T, T), BF16)] * 4,
            f32(2, 8, T, 512),
            f32(8, T, 512),
            f32(T // 2, 512), f32(T // 2, 512), f32(3, T, 512), f32(3, T, 512),
            f32(2, T, 512), f32(2, 32, 512), f32(2, T, 512), f32(4, 2, T, 512),
            pltpu.VMEM((3, 8, 32, T), BF16),
            f32(2, 2, 32, 512), f32(2, 32, 512), f32(7, 8, 512), f32(8, 512), f32(32, 512),
            f32(2, T, 512), f32(T, T),
            f32(32, 256), f32(8, 256), f32(2, 8, 256), f32(2, 32, 256), f32(2, T, 256),
            f32(T, 256),
            f32(3 * T, T), f32(T, T),
            dma((3, 4)), dma((3, 4)), dma((4,)), dma((4,)), dma((2, 4)), dma((2, 4)),
            dma((3,)), dma((2,)), dma((3,)), dma, dma((3,)), dma,
            dma((3,)), dma((3,)), dma((3,)), dma((3,)),
            dma((3,)), dma((3,)), dma, dma, dma((7,)), dma((7,)), dma((3,)), dma((3,)),
            dma((3,)), dma((3,)),
            dma((3,)), dma((2,)), dma((3,)), dma,
            dma((3,)), dma, dma((3,)), dma, dma((3,)), dma, dma((3,)), dma((2,)),
            dma((3,)), dma((3,)), dma((3,)), dma((3,)), dma((3,)), dma,
        ],
        compiler_params=pltpu.CompilerParams(
            collective_id=0, has_side_effects=True, vmem_limit_bytes=VMEM_LIMIT
        ),
        name="solve",
    )(tiles, factor, coupling, bem)


def local(inverse_factor, coupling, boundary_tiles, bem_block):
    return solve(boundary_tiles, inverse_factor[0], coupling[0], bem_block[0, 0])[None, None]


def solution(mesh):
    placed = (
        P(("fem", "row", "col"), None, None),
        P(("fem", "row", "col"), None, None),
        P(),
        P(None, ("fem", "row"), None, "col"),
    )
    return jax.shard_map(
        local,
        mesh=mesh,
        in_specs=placed,
        out_specs=P(None, ("fem", "row"), None, "col"),
        check_vma=False,
    )
```

```python
import jax
import jax.numpy as jnp
from jax import lax
from jax.experimental import pallas as pl
from jax.experimental.pallas import tpu as pltpu
from jax.sharding import PartitionSpec as P

MESH = pl.DeviceIdType.MESH
F32 = jnp.float32
BF16 = jnp.bfloat16
T = 128
VMEM_LIMIT = 60 * 1024 * 1024


def highest(left, right):
    return jnp.dot(left, right, precision=lax.Precision.HIGHEST, preferred_element_type=F32)


def eliminate_part(work, unit, part, last):
    lanes = lax.broadcasted_iota(jnp.int32, (1, T), 1)
    top = part * 32
    count = last - top
    place = lax.broadcasted_iota(jnp.int32, (count, 1), 0) + top

    def block(step, carry):
        start = pl.multiple_of(top + step * 8, 8)
        for t in range(8):
            row = work[pl.ds(start + t, 1), :]
            unit_row = unit[pl.ds(start + t, 1), :]
            inverse_pivot = 1.0 / row[:, t : t + 1]
            below = place > start + t
            body = work[top:last, :]
            scaled = jnp.where(below, body[:, t : t + 1] * inverse_pivot, 0.0)
            right = jnp.where((lanes > t) & (lanes < T - start), row, 0.0)
            work[top:last, :] = jnp.where((lanes == t) & below, scaled, body - scaled * right)
            unit[top:T, :] = unit[top:T, :] - scaled[: T - top] * unit_row
        work[top:last, :] = pltpu.roll(work[top:last, :], T - 8, 1)
        return carry

    lax.fori_loop(0, 4, block, 0)


def turn_back(work):
    for part in range(3):
        cut = slice(part * 32, (part + 1) * 32)
        work[cut, :] = pltpu.roll(work[cut, :], (part + 1) * 32, 1)


def solve_kernel(
    tiles_ref, factor_ref, coupling_ref, bem_ref,
    out_ref,
    slot_ref, weight_ref, factor, coupling, coupled, compact, dense_ref, f_sem, k_sem,
    recv0, recv1, recv2, recv3, acc, other, plus0, minus0, plus, minus,
    xpart, ypart, zpart, panel,
    prow, psum, pother, pz, piece, pa32, pa, atile,
    dy32, d8, gq, g32, diag, cols,
    work, unit,
    y_send, y_recv, c_send, c_recv, r_send, r_recv,
    px_send, px_recv, py_send, py_recv, pz_send, pz_recv, gy_send, gy_recv, gx_send, gx_recv,
    b1_send, b1_recv, b2_send, b2_recv, b3_send, b3_recv, b4_send, b4_recv, b5_send, b5_recv,
    b6_send, b6_recv, at_send, at_recv,
    e1_send, e1_recv, e2_send, e2_recv, q0_send, q0_recv, q1_send, q1_recv,
    q2_send, q2_recv, q3_send, q3_recv, a_send, a_recv,
):
    f = lax.axis_index("fem")
    r = lax.axis_index("row")
    c = lax.axis_index("col")
    zh, y = f // 4, f % 4
    zl, core = c // 2, c % 2
    z = zh * 2 + zl
    three = (1, 2, 3)
    recv = (recv0, recv1, recv2, recv3)

    def at_y(d):
        return (zh * 4 + (y + d) % 4, r, c)

    def at_z(d):
        to = (z + d) % 8
        return ((to // 2) * 4 + y, r, (to % 2) * 2 + core)

    def at_zh(d):
        return (((zh + d) % 4) * 4 + y, r, c)

    def at_x(d):
        return (f, (r + d) % 4, c)

    def at_col(d):
        return (f, r, (c + d) % 4)

    partner = (f, r, c + 1 - 2 * core)

    def copy(src, dst, send, recv_sem, to):
        return pltpu.make_async_remote_copy(
            src_ref=src, dst_ref=dst, send_sem=send, recv_sem=recv_sem,
            device_id=to, device_id_type=MESH,
        )

    def arrive(dst, recv_sem):
        copy(dst, dst, recv_sem, recv_sem, at_x(1)).wait_recv()

    def start(copies):
        for one in copies:
            one.start()

    def rows_of(index, count):
        return pl.ds(pl.multiple_of(index * count, count), count)

    order, width = coupling.shape
    step = 256
    loads = []
    for i in range(order // step):
        block = pl.ds(i * step, step)
        left_part = pl.ds(0, (i + 1) * step)
        loads.append(
            (
                pltpu.make_async_copy(
                    factor_ref.at[block, left_part], factor.at[block, left_part], f_sem.at[i]
                ),
                pltpu.make_async_copy(coupling_ref.at[block], coupling.at[block], k_sem.at[i]),
            )
        )
        start(loads[i])

    barrier = pltpu.get_barrier_semaphore()
    greet = [at_y(d) for d in three] + [at_z(d) for d in range(1, 8)]
    greet += [at_x(d) for d in three] + [at_col(d) for d in three]
    for to in greet:
        pl.semaphore_signal(barrier, inc=1, device_id=to, device_id_type=MESH)
    pl.semaphore_wait(barrier, len(greet))

    in_panel = r < 2
    is_root = (f == 0) & in_panel
    mine = r % 2

    b1 = [
        copy(
            dense_ref.at[0, :, rows_of((y + d) % 4, 32)], prow.at[d - 1],
            b1_send.at[d - 1], b1_recv.at[d - 1], at_y(d),
        )
        for d in three
    ]
    e1 = [
        copy(
            bem_ref.at[pl.ds(d * 32, 32), pl.ds(0, 256)], dy32, e1_send.at[d - 1], e1_recv,
            (d, r, c),
        )
        for d in three
    ]
    e2 = [
        copy(
            dy32.at[rows_of((zh + d) % 4, 8)], d8, e2_send.at[d - 1], e2_recv, at_zh(d)
        )
        for d in three
    ]
    a_copies = [
        copy(bem_ref.at[:, pl.ds(0, 256)], cols, a_send.at[d - 1], a_recv, at_col(d))
        for d in three
    ]
    px = [
        copy(
            bem_ref.at[:, rows_of((r + d) % 4, 512)], xpart.at[mine],
            px_send.at[d - 1], px_recv.at[mine], at_x(d),
        )
        for d in three
    ]

    @pl.when(is_root)
    def _():
        @pl.when(c == 0)
        def _():
            start(e1)
            dy32[...] = bem_ref[0:32, 0:256]

        start(px)
        xpart[mine] = bem_ref[:, rows_of(mine, 512)]

    @pl.when(c == 0)
    def _():
        start(a_copies)
        cols[...] = bem_ref[:, 0:256]

    rounds = (2, 1, 3, 0)
    tile_row = [(zh + turn) % 4 for turn in rounds]
    y_copies = [
        [
            copy(
                dense_ref.at[tile_row[k] * 4 + (y + d) % 4], recv[k].at[d - 1],
                y_send.at[d - 1, k], y_recv.at[d - 1, k], at_y(d),
            )
            for d in three
        ]
        for k in range(4)
    ]

    py = [
        copy(xpart.at[:, pl.ds(d * 32, 32)], ypart, py_send.at[d - 1], py_recv, (d, r, c))
        for d in three
    ]
    pzs = [copy(ypart, ypart, pz_send.at[d - 1], pz_recv, at_zh(d)) for d in three]

    gy = [
        copy(ypart, zpart.at[:, rows_of(y, 32)], gy_send.at[d - 1], gy_recv.at[d - 1], at_y(d))
        for d in three
    ]
    gx = [
        copy(zpart, panel.at[r], gx_send.at[d - 1], gx_recv.at[d - 1], at_x(d)) for d in three
    ]

    for d in range(4):
        source = ((zh * 4 + (y + 4 - d) % 4) * 4 + r) * 4 + c
        listed = [tiles_ref[source, k] for k in range(8)]

        def look(b, carry):
            slot = jnp.int32(0)
            weight = jnp.float32(0.0)
            for k in range(8):
                slot = jnp.where(listed[k] == b, k, slot)
                weight = jnp.where(listed[k] == b, jnp.float32(1.0), weight)
            slot_ref[d * 16 + b] = slot
            weight_ref[d * 16 + b] = weight
            return carry

        lax.fori_loop(0, 16, look, 0)

    for i in range(order // step):
        for one in loads[i]:
            one.wait()
        for n in range(width // 512):
            coupled[i * step : (i + 1) * step, n * 512 : (n + 1) * 512] = jnp.dot(
                factor[i * step : (i + 1) * step, : (i + 1) * step],
                coupling[: (i + 1) * step, n * 512 : (n + 1) * 512],
                preferred_element_type=F32,
            ).astype(BF16)

    @pl.when(in_panel & (c == 0))
    def _():
        @pl.when(zh == 0)
        def _():
            @pl.when(y != 0)
            def _():
                arrive(dy32, e1_recv)

            start(e2)
            d8[...] = dy32[0:8]

    @pl.when(f == 0)
    def _():
        for m in range(2):
            @pl.when(r != m)
            def _():
                arrive(xpart.at[m], px_recv.at[m])

        start(py)
        ypart[...] = xpart[:, 0:32]

    for pair in range(width // step):
        for n in range(width // 512):
            both = lax.dot_general(
                coupled[:, pair * step : (pair + 1) * step],
                coupled[:, n * 512 : (n + 1) * 512],
                (((0,), (0,)), ((), ())),
                preferred_element_type=F32,
            ).astype(BF16)
            for i in range(step // T):
                for j in range(512 // T):
                    compact[pair * (step // T) + i, n * (512 // T) + j] = both[
                        i * T : (i + 1) * T, j * T : (j + 1) * T
                    ]

    dense_ref[0] = compact[slot_ref[0]]

    @pl.when(in_panel)
    def _():
        start(b1)

    def place(b, carry):
        dense_ref[b] = compact[slot_ref[b]]
        return carry

    lax.fori_loop(1, 16, place, 0)
    start(y_copies[0])
    b2 = copy(psum.at[1], pother, b2_send, b2_recv, partner)
    b3 = [
        copy(
            psum.at[0, ((z + d) % 8) % 2, rows_of(((z + d) % 8) // 2, 8)], pz.at[d - 1],
            b3_send.at[d - 1], b3_recv.at[d - 1], at_z(d),
        )
        for d in range(1, 8)
    ]

    @pl.when(in_panel)
    def _():
        for one in b1:
            one.wait_recv()

        def add_row(b4, carry):
            for i in range(4):
                b = b4 * 4 + i
                total = compact[slot_ref[0], slot_ref[b], rows_of(y, 32)].astype(F32) * (
                    weight_ref[b] * weight_ref[0]
                )
                for d in three:
                    total += prow[d - 1, slot_ref[d * 16 + b]].astype(F32) * (
                        weight_ref[d * 16 + b] * weight_ref[d * 16]
                    )
                psum[(b4 % 2 + core) % 2, b4 // 2, :, i * T : (i + 1) * T] = total
            return carry

        lax.fori_loop(0, 4, add_row, 0)
        b2.start()

    @pl.when(in_panel)
    def _():
        b2.wait_recv()
        psum[0] = psum[0] + pother[...]
        start(b3)

    @pl.when(zh == 0)
    def _():
        @pl.when(y != 0)
        def _():
            arrive(ypart, py_recv)

        start(pzs)

    start(y_copies[1])

    q0 = [copy(gq.at[mine], gq.at[mine], q0_send.at[d - 1], q0_recv, at_col(d)) for d in three]
    q1 = [
        copy(gq.at[mine], gq.at[mine], q1_send.at[d - 1], q1_recv.at[mine], at_x(d))
        for d in three
    ]
    b4 = [
        copy(piece, pa32.at[rows_of(zh, 8)], b4_send.at[d - 1], b4_recv.at[d - 1], at_zh(d))
        for d in three
    ]

    @pl.when(in_panel)
    def _():
        for one in b3:
            one.wait_recv()
        total = psum[0, zl, rows_of(zh, 8)]
        for d in range(7):
            total += pz[d]
        piece[...] = total
        start(b4)
        pa32[rows_of(zh, 8)] = total

        @pl.when(c == 0)
        def _():
            @pl.when(zh != 0)
            def _():
                arrive(d8, e2_recv)

            for m in range(2):
                @pl.when(r == m)
                def _():
                    gq[m, :, (1 - m) * T : (2 - m) * T] = d8[:, (1 - m) * T : (2 - m) * T]
                    gq[m, :, m * T : (m + 1) * T] = d8[:, m * T : (m + 1) * T] + total[:, 0:T]

            start(q0)

        @pl.when(c != 0)
        def _():
            arrive(gq.at[mine], q0_recv)

        start(q1)

    q2 = [
        copy(gq, g32.at[:, rows_of(zh, 8)], q2_send.at[d - 1], q2_recv.at[d - 1], at_zh(d))
        for d in three
    ]
    q3 = [
        copy(g32, diag.at[:, rows_of(y, 32)], q3_send.at[d - 1], q3_recv.at[d - 1], at_y(d))
        for d in three
    ]
    b5 = [
        copy(pa32, pa.at[mine, rows_of(y, 32)], b5_send.at[d - 1], b5_recv.at[d - 1], at_y(d))
        for d in three
    ]
    b6 = [
        copy(pa.at[mine], pa.at[mine], b6_send.at[d - 1], b6_recv.at[mine], at_x(d))
        for d in three
    ]
    tile_lanes = rows_of(f % 4, T)
    at_copies = [
        copy(pa.at[mine, :, tile_lanes], atile, at_send.at[d - 1], at_recv, at_col(d))
        for d in three
    ]
    for m in range(2):
        @pl.when(r != m)
        def _():
            arrive(gq.at[m], q1_recv.at[m])

    start(q2)
    g32[:, rows_of(zh, 8)] = gq[...]

    @pl.when(in_panel)
    def _():
        for one in b4:
            one.wait_recv()
        start(b5)
        pa[mine, rows_of(y, 32)] = pa32[...]

    for one in q2:
        one.wait_recv()
    start(q3)
    diag[:, rows_of(y, 32)] = g32[...]
    @pl.when(zh != 0)
    def _():
        arrive(ypart, pz_recv)

    start(gy)
    zpart[:, rows_of(y, 32)] = ypart[...]

    start(y_copies[2])
    start(y_copies[3])

    swaps = [
        copy(
            acc.at[1, rows_of(tile_row[k], 2)], other.at[rows_of(tile_row[k], 2)],
            c_send.at[k], c_recv.at[k], partner,
        )
        for k in range(4)
    ]

    def add_round(k):
        for one in y_copies[k]:
            one.wait_recv()
        q = tile_row[k]
        row = q * 4 + y

        def gather(b4, carry):
            for i in range(4):
                b = b4 * 4 + i
                total = compact[slot_ref[row], slot_ref[b]].astype(F32) * (
                    weight_ref[b] * weight_ref[row]
                )
                for d in three:
                    total += recv[k][d - 1, slot_ref[d * 16 + b]].astype(F32) * (
                        weight_ref[d * 16 + b] * weight_ref[d * 16 + row]
                    )
                acc[(b4 % 2 + core) % 2, q * 2 + b4 // 2, :, i * T : (i + 1) * T] = total
            return carry

        lax.fori_loop(0, 4, gather, 0)
        swaps[k].start()

    half = T // 2
    ring = []

    def hop(src, dst, lane, d):
        one = copy(src, dst, r_send.at[lane, d], r_recv.at[lane, d], at_z(1 + 6 * lane))
        one.start()
        ring.append(one)
        return one

    def first_hop():
        swaps[0].wait_recv()
        far = (z + 4) % 8
        acc[0, far] = acc[0, far] + other[far]
        return (
            hop(acc.at[0, far, pl.ds(0, half)], plus0, 0, 0),
            hop(acc.at[0, far, pl.ds(half, half)], minus0, 1, 0),
        )

    def next_hop(d, up, down):
        zp = (z + d) % 8
        zm = (z + 8 - d) % 8
        acc[0, zp] = acc[0, zp] + other[zp]
        acc[0, zm] = acc[0, zm] + other[zm]
        up.wait_recv()
        if d == 3:
            acc[0, zp, 0:half] = acc[0, zp, 0:half] + plus0[...]
        else:
            acc[0, zp] = acc[0, zp] + plus[2 - d]
        up = hop(acc.at[0, zp], plus.at[3 - d], 0, 4 - d)
        down.wait_recv()
        if d == 3:
            acc[0, zm, half:T] = acc[0, zm, half:T] + minus0[...]
        else:
            acc[0, zm] = acc[0, zm] + minus[2 - d]
        down = hop(acc.at[0, zm], minus.at[3 - d], 1, 4 - d)
        return up, down

    add_round(0)

    @pl.when(in_panel)
    def _():
        for one in b5:
            one.wait_recv()
        start(b6)

        @pl.when(c == f // 4)
        def _():
            start(at_copies)
            atile[...] = pa[mine, :, tile_lanes]

    for one in q3:
        one.wait_recv()

    @pl.when(c != 0)
    def _():
        arrive(cols, a_recv)

    @pl.when(in_panel)
    def _():
        @pl.when(c != f // 4)
        def _():
            arrive(atile, at_recv)

        turned = atile[...].T
        for m in range(2):
            @pl.when(r == m)
            def _():
                cols[:, m * T : (m + 1) * T] = cols[:, m * T : (m + 1) * T] + turned

    identity = (
        lax.broadcasted_iota(jnp.int32, (T, T), 0) == lax.broadcasted_iota(jnp.int32, (T, T), 1)
    ).astype(F32)
    work[0:T, :] = diag[0, :, 0:T]
    work[T : 2 * T, :] = diag[1, :, 0:T]
    work[2 * T : 3 * T, :] = cols[:, 0:T]
    unit[...] = identity
    eliminate_part(work, unit, 0, 3 * T)
    for one in gy:
        one.wait_recv()
    start(gx)
    panel[r] = zpart[...]
    up, down = first_hop()
    eliminate_part(work, unit, 1, 3 * T)
    add_round(1)
    eliminate_part(work, unit, 2, 3 * T)
    eliminate_part(work, unit, 3, 3 * T)
    turn_back(work)
    first = work[...]
    first_inv = unit[...]
    upper = highest(first_inv, diag[0, :, T:256])
    add_round(2)
    swaps[1].wait_recv()
    swaps[2].wait_recv()
    up, down = next_hop(3, up, down)
    work[0:T, :] = diag[1, :, T:256] - highest(first[T : 2 * T], upper)
    work[T : 2 * T, :] = cols[:, T:256] - highest(first[2 * T :], upper)
    unit[...] = identity
    eliminate_part(work, unit, 0, 2 * T)
    eliminate_part(work, unit, 1, 2 * T)
    up, down = next_hop(2, up, down)
    eliminate_part(work, unit, 2, 2 * T)
    add_round(3)
    eliminate_part(work, unit, 3, 2 * T)
    turn_back(work)
    swaps[3].wait_recv()
    up, down = next_hop(1, up, down)

    second = work[0 : 2 * T, :]
    second_inv = unit[...]
    corner = -highest(second_inv, highest(first[T : 2 * T], first_inv))
    lower = second[T:]
    left = jnp.where(
        is_root,
        jnp.where(r == 0, first_inv, corner),
        -(highest(first[2 * T :], first_inv) + highest(lower, corner)),
    )
    right = jnp.where(
        is_root,
        jnp.where(r == 0, jnp.zeros_like(second_inv), second_inv),
        -highest(lower, second_inv),
    )
    keep = jnp.where(is_root, 0.0, 1.0).astype(F32)
    for one in gx:
        one.wait_recv()
    for m in range(2):
        @pl.when(r != m)
        def _():
            arrive(pa.at[m], b6_recv.at[m])

    for n in range(4):
        for m in range(2):
            panel[n, m, :, m * T : (m + 1) * T] = (
                panel[n, m, :, m * T : (m + 1) * T] + pa[m, :, n * T : (n + 1) * T]
            )
    for n in range(4):
        cut = pl.ds(n * 512, 512)
        out_ref[:, cut] = (
            bem_ref[:, cut] * keep + highest(left, panel[n, 0]) + highest(right, panel[n, 1])
        )

    up.wait_recv()
    down.wait_recv()
    for i in range(4):
        lanes = pl.ds(pl.multiple_of((i * 4 + r) * T, T), T)
        part = pl.ds(i * T, T)
        out_ref[:, lanes] = out_ref[:, lanes] + keep * (
            acc[0, z, :, part] + other[z, :, part] + plus[2, :, part] + minus[2, :, part]
        )

    @pl.when(c == 0)
    def _():
        out_ref[:, 0:T] = jnp.where(
            is_root, jnp.where(r == 0, first[0:T], first[T : 2 * T]), first[2 * T :]
        )
        out_ref[:, T:256] = jnp.where(
            is_root, jnp.where(r == 0, upper, second[0:T]), lower
        )

    def sent(copies):
        for one in copies:
            one.wait_send()

    sent(ring + swaps + gy + gx + q2 + q3)
    for k in range(4):
        sent(y_copies[k])

    @pl.when(in_panel)
    def _():
        sent(b1 + [b2] + b3 + b4 + b5 + b6 + q1)

        @pl.when(c == 0)
        def _():
            sent(q0)

            @pl.when(zh == 0)
            def _():
                sent(e2)

        @pl.when(f == 0)
        def _():
            sent(px)

            @pl.when(c == 0)
            def _():
                sent(e1)

        @pl.when(c == f // 4)
        def _():
            sent(at_copies)

    @pl.when(c == 0)
    def _():
        sent(a_copies)

    @pl.when(f == 0)
    def _():
        sent(py)

    @pl.when(zh == 0)
    def _():
        sent(pzs)


def solve(tiles, factor, coupling, bem):
    vmem = pl.BlockSpec(memory_space=pltpu.VMEM)
    smem = pl.BlockSpec(memory_space=pltpu.SMEM)
    dma = pltpu.SemaphoreType.DMA
    f32 = lambda *shape: pltpu.VMEM(shape, F32)
    return pl.pallas_call(
        solve_kernel,
        out_shape=jax.ShapeDtypeStruct(bem.shape, F32),
        in_specs=[smem, pl.BlockSpec(memory_space=pl.ANY), pl.BlockSpec(memory_space=pl.ANY), vmem],
        out_specs=vmem,
        scratch_shapes=[
            pltpu.SMEM((64,), jnp.int32), pltpu.SMEM((64,), F32),
            pltpu.VMEM(factor.shape, BF16), pltpu.VMEM(coupling.shape, BF16),
            pltpu.VMEM(coupling.shape, BF16),
            pltpu.VMEM((8, 8, T, T), BF16), pltpu.VMEM((16, 8, T, T), BF16),
            dma((6,)), dma((6,)),
            *[pltpu.VMEM((3, 8, T, T), BF16)] * 4,
            f32(2, 8, T, 512),
            f32(8, T, 512),
            f32(T // 2, 512), f32(T // 2, 512), f32(3, T, 512), f32(3, T, 512),
            f32(2, T, 512), f32(2, 32, 512), f32(2, T, 512), f32(4, 2, T, 512),
            pltpu.VMEM((3, 8, 32, T), BF16),
            f32(2, 2, 32, 512), f32(2, 32, 512), f32(7, 8, 512), f32(8, 512), f32(32, 512),
            f32(2, T, 512), f32(T, T),
            f32(32, 256), f32(8, 256), f32(2, 8, 256), f32(2, 32, 256), f32(2, T, 256),
            f32(T, 256),
            f32(3 * T, T), f32(T, T),
            dma((3, 4)), dma((3, 4)), dma((4,)), dma((4,)), dma((2, 4)), dma((2, 4)),
            dma((3,)), dma((2,)), dma((3,)), dma, dma((3,)), dma,
            dma((3,)), dma((3,)), dma((3,)), dma((3,)),
            dma((3,)), dma((3,)), dma, dma, dma((7,)), dma((7,)), dma((3,)), dma((3,)),
            dma((3,)), dma((3,)),
            dma((3,)), dma((2,)), dma((3,)), dma,
            dma((3,)), dma, dma((3,)), dma, dma((3,)), dma, dma((3,)), dma((2,)),
            dma((3,)), dma((3,)), dma((3,)), dma((3,)), dma((3,)), dma,
        ],
        compiler_params=pltpu.CompilerParams(
            collective_id=0, has_side_effects=True, vmem_limit_bytes=VMEM_LIMIT
        ),
        name="solve",
    )(tiles, factor, coupling, bem)


def local(inverse_factor, coupling, boundary_tiles, bem_block):
    return solve(boundary_tiles, inverse_factor[0], coupling[0], bem_block[0, 0])[None, None]


def solution(mesh):
    placed = (
        P(("fem", "row", "col"), None, None),
        P(("fem", "row", "col"), None, None),
        P(),
        P(None, ("fem", "row"), None, "col"),
    )
    return jax.shard_map(
        local,
        mesh=mesh,
        in_specs=placed,
        out_specs=P(None, ("fem", "row"), None, "col"),
        check_vma=False,
    )
```
